128 devices in a mesh: layer: 4 (over x_hi, core), example: 32 (over z, x_lo, y).
Axes of the slice: x: 4 (x_hi: 2, x_lo: 2; x = x_hi * 2 + x_lo), y: 4, z: 4, core: 2. Of those that a mesh axis runs over, the one named last changes fastest.
Arguments:
- train_features: bfloat16 [4, 49152, 4096], P('layer', 'example'), may hold values from -0.046875 to 0.046875
- query_codes: bfloat16 [4, 2048, 4096], P('layer', 'example'), may hold values from -512 to 512
- query_exponents: int32 [4, 2048], P('layer', 'example'), may hold values from 6 to 10
Outputs:
- scores: float32 [2048, 49152], P('layer', 'example')
The draws below stay inside these ranges and needn't reach their ends.
All inputs are finite; a program needn't handle non-finite values.
Results may differ from the reference program's by a relative error of at most 0.0003.
Values may be sent and summed in bfloat16 or wider, within the bound.
No kernel may reach another device: no remote copies, remote signals or barrier semaphores. Data moves between devices by JAX's collectives and lax.ppermute only.
A program may use at most 128 MiB of HBM per device.

```python
import jax
import jax.numpy as jnp
from jax import lax

P_SIZE = 4096
QUERIES = 2048
LAYERS = 4
TRAIN = 49152


def set_ends(result, stream_key, low, top_value):
    extent = result.shape
    place = [jax.random.randint(jax.random.fold_in(stream_key, axis), (), 0, extent[axis]) for axis in range(len(extent))]
    result = result.at[tuple(place)].set(low)
    longest = extent.index(max(extent))
    place[longest] = (place[longest] + 1) % extent[longest]
    return result.at[tuple(place)].set(top_value)


def shard_levels(key, dims, pieces, smallest, top_value):
    loudness, own = 1.0, jax.random.fold_in(key, 6)
    for dim, parts in pieces:
        steps = jnp.exp(jax.random.uniform(jax.random.fold_in(own, dim), (parts,), jnp.float32, smallest / len(pieces), top_value / len(pieces)))
        loudness = loudness * jnp.repeat(steps, dims[dim] // parts).reshape([-1 if axis == dim else 1 for axis in range(len(dims))])
    return loudness


def centred(rng, shape, width, most, cuts=(), dtype=jnp.bfloat16):
    result = jax.random.normal(rng, shape, jnp.float32) * width
    if len(cuts) > 0:
        result = shard_levels(rng, shape, cuts, -0.22, 0.18) * result
    return jnp.clip(result, min=-most, max=most).astype(dtype)


def setup_inputs(seed: int = 0) -> dict:
    key_of = jax.random.split(jax.random.key(seed), 4)
    return {
        "train_features": centred(key_of[0], (LAYERS, TRAIN, P_SIZE), (LAYERS * P_SIZE) ** -0.5, 0.046875, ((0, 4), (1, 32))),
        "query_codes": centred(key_of[1], (LAYERS, QUERIES, P_SIZE), 128.0, 512.0, ((0, 4), (1, 32))),
        "query_exponents": set_ends(jax.random.randint(key_of[2], (LAYERS, QUERIES), 6, 11), jax.random.fold_in(key_of[2], 1), 6, 10).astype(jnp.int32),
    }


def reference(train_features, query_codes, query_exponents):
    row_scale = jnp.exp2(-query_exponents.astype(jnp.float32))
    dequant = (query_codes.astype(jnp.float32) * row_scale[:, :, None]).astype(jnp.bfloat16)

    def add_layer(totals, layer_pair):
        train_layer, query_layer = layer_pair
        product = jnp.dot(query_layer.astype(jnp.float32), train_layer.astype(jnp.float32).T,
                          precision=lax.Precision.HIGHEST, preferred_element_type=jnp.float32)
        return totals + product, None

    initial = jnp.zeros((query_codes.shape[1], train_features.shape[1]), jnp.float32)
    scores, _ = lax.scan(add_layer, initial, (train_features, dequant))
    return scores
```

```python
import jax
import jax.numpy as jnp
from jax import lax
from jax.sharding import PartitionSpec as P

BOTH = ("layer", "example")


def moves(step):
    pairs = []
    for x in range(4):
        for core in range(2):
            for z in range(4):
                for y in range(4):
                    tx, tc, tz, ty = step(x, core, z, y)
                    pairs.append((place(x, core, z, y), place(tx % 4, tc % 2, tz % 4, ty % 4)))
    return pairs


def place(x, core, z, y):
    return (2 * (x // 2) + core) * 32 + (2 * z + x % 2) * 4 + y


FIRST_UP = moves(lambda x, c, z, y: (x, c, z + c, y + 1 - c))
FIRST_DOWN = moves(lambda x, c, z, y: (x, c, z - c, y - 1 + c))
SECOND_UP = moves(lambda x, c, z, y: (x, c, z + 1 - c, y + c))
SECOND_DOWN = moves(lambda x, c, z, y: (x, c, z - 1 + c, y - c))
PAIR = moves(lambda x, c, z, y: (x ^ 1, c, z, y))
CORE = moves(lambda x, c, z, y: (x, c + 1, z, y))
ACROSS = moves(lambda x, c, z, y: (x + 2, c, z, y))


def send(value, pairs):
    return lax.ppermute(value, BOTH, pairs)


def narrow(block):
    peak = jnp.maximum(jnp.max(jnp.abs(block), axis=0, keepdims=True), 1e-30)
    power = 13.0 - jnp.floor(jnp.log2(peak))
    scaled = (block * jnp.exp2(power)).astype(jnp.float16)
    return jnp.concatenate([scaled, jnp.broadcast_to(power, (8, block.shape[1])).astype(jnp.float16)], 0)


def widen(message):
    return message[:-8].astype(jnp.float32) * jnp.exp2(-message[-8:-7].astype(jnp.float32))


def shards(train_features, query_codes, query_exponents):
    layer, example = lax.axis_index("layer"), lax.axis_index("example")
    half, core = layer // 2, layer % 2
    z, low, y = example // 8, (example // 4) % 2, example % 4
    train = train_features[0]
    row_scale = jnp.exp2(-query_exponents[0].astype(jnp.float32))
    own = (query_codes[0].astype(jnp.float32) * row_scale[:, None]).astype(jnp.bfloat16)

    def by_core(zero, one):
        return jnp.where(core == 0, zero, one)

    def times(blocks):
        return lax.dot_general(
            jnp.concatenate(blocks, 0), train, (((1,), (1,)), ((), ())), preferred_element_type=jnp.float32
        ).reshape(len(blocks), 128, -1)

    q = {}
    pair = send(own, PAIR)
    below, above = send(own, FIRST_UP), send(own, FIRST_DOWN)
    q[0, 0] = jnp.concatenate([own, pair], 0)
    below_pair, above_pair = send(pair, FIRST_UP), send(pair, FIRST_DOWN)
    far, far_pair = send(below, FIRST_UP), send(above_pair, FIRST_DOWN)
    q[3, 0] = jnp.concatenate([below, below_pair], 0)
    q[1, 0] = jnp.concatenate([above, above_pair], 0)
    q[2, 0] = jnp.concatenate([far, far_pair], 0)
    q[0, 3], q[0, 1] = send(q[0, 0], SECOND_UP), send(q[0, 0], SECOND_DOWN)
    q[3, 3], q[1, 1] = send(q[3, 0], SECOND_UP), send(q[1, 0], SECOND_DOWN)
    third, q[3, 1] = send(by_core(q[0, 3], q[2, 0]), SECOND_UP), send(q[3, 0], SECOND_DOWN)
    q[1, 3], q[2, 1] = send(q[1, 0], SECOND_UP), send(q[2, 0], SECOND_DOWN)
    q[3, 2], q[1, 2] = send(q[3, 3], SECOND_UP), send(q[1, 1], SECOND_DOWN)
    sixth, q[2, 2] = send(by_core(q[2, 0], q[0, 3]), SECOND_UP), send(q[2, 1], SECOND_DOWN)

    out = jnp.zeros((2, 4, 64, train.shape[0]), jnp.float32)

    def reduce(out, dy, partial, spots):
        def plane(target):
            return lax.dynamic_index_in_dim(partial, spots((target - z) % 4), 0, keepdims=False)

        got = send(jnp.stack([plane(1 - core), plane(3 - core)]), CORE)
        other = plane(2 * (1 - half) + core) + lax.dynamic_index_in_dim(got, 1 - half, 0, keepdims=False)
        far_sum = send(narrow(other), ACROSS)
        mine = plane(2 * half + core) + lax.dynamic_index_in_dim(got, half, 0, keepdims=False)
        total = mine + widen(far_sum)
        column = (y + dy) % 4
        out = lax.dynamic_update_slice(out, total[None, None, :64], (low, column, 0, 0))
        return lax.dynamic_update_slice(out, total[None, None, 64:], (1 - low, column, 0, 0))

    straight = lambda spot: spot
    out = reduce(out, 0, times([q[0, 0], by_core(q[0, 1], q[1, 0]), by_core(third, q[2, 0]), by_core(q[0, 3], q[3, 0])]), straight)
    out = reduce(out, 1, times([by_core(q[1, 0], q[0, 1]), q[1, 1], by_core(q[1, 2], q[2, 1]), by_core(q[1, 3], q[3, 1])]), straight)
    out = reduce(out, 3, times([by_core(q[3, 0], q[0, 3]), by_core(q[3, 1], q[1, 3]), by_core(q[3, 2], third), q[3, 3]]), straight)
    early = times([by_core(q[2, 0], q[3, 2]), by_core(q[2, 1], q[1, 2])])
    late = times([q[2, 2], sixth])
    out = reduce(out, 2, jnp.concatenate([early, late], 0), lambda spot: by_core(spot, jnp.array([3, 1, 2, 0])[spot]))
    return out.reshape(512, -1)


def solution(mesh):
    in_specs = (P("layer", "example", None), P("layer", "example", None), P("layer", "example"))
    out_specs = P("layer", "example")
    return jax.shard_map(shards, mesh=mesh, in_specs=in_specs, out_specs=out_specs, check_vma=False)
```

```python
import functools

import jax
import jax.numpy as jnp
from jax import lax
from jax.experimental import pallas as pl
from jax.experimental.pallas import tpu as pltpu
from jax.sharding import PartitionSpec as P

BOTH = ("layer", "example")


def moves(step):
    pairs = []
    for x in range(4):
        for core in range(2):
            for z in range(4):
                for y in range(4):
                    tx, tc, tz, ty = step(x, core, z, y)
                    pairs.append((place(x, core, z, y), place(tx % 4, tc % 2, tz % 4, ty % 4)))
    return pairs


def place(x, core, z, y):
    return (2 * (x // 2) + core) * 32 + (2 * z + x % 2) * 4 + y


FIRST_UP = moves(lambda x, c, z, y: (x, c, z + c, y + 1 - c))
FIRST_DOWN = moves(lambda x, c, z, y: (x, c, z - c, y - 1 + c))
SECOND_UP = moves(lambda x, c, z, y: (x, c, z + 1 - c, y + c))
SECOND_DOWN = moves(lambda x, c, z, y: (x, c, z - 1 + c, y - c))
PAIR = moves(lambda x, c, z, y: (x ^ 1, c, z, y))
CORE = moves(lambda x, c, z, y: (x, c + 1, z, y))
ACROSS = moves(lambda x, c, z, y: (x + 2, c, z, y))


def send(value, pairs):
    return lax.ppermute(value, BOTH, pairs)


VMEM = 40 * 2**20
TILE = 512


def product_kernel(choices, count, core, *refs):
    blocks, train, out, rows, sems = refs[:count], *refs[count:]

    @pl.when(pl.program_id(0) == 0)
    def _():
        for slot, pair in enumerate(choices):
            for number, choice in enumerate(pair):

                @pl.when(core[0] == number)
                def _(slot=slot, choice=choice):
                    pltpu.make_async_copy(blocks[choice], rows.at[pl.ds(slot * 128, 128)], sems.at[slot]).start()

        for slot in range(len(choices)):
            pltpu.make_async_copy(blocks[0], rows.at[pl.ds(slot * 128, 128)], sems.at[slot]).wait()

    out[...] = lax.dot_general(rows[...], train[...], (((1,), (1,)), ((), ())), preferred_element_type=jnp.float32)


def products(core, pairs, train):
    depth, width = train.shape[1], train.shape[0]
    blocks, choices = [], []
    for pair in pairs:
        spots = []
        for block in pair:
            found = [n for n, known in enumerate(blocks) if known is block]
            if not found:
                blocks.append(block)
            spots.append(found[0] if found else len(blocks) - 1)
        choices.append(spots)
    rows = 128 * len(pairs)
    return pl.pallas_call(
        functools.partial(product_kernel, choices, len(blocks)),
        grid=(width // TILE,),
        in_specs=[pl.BlockSpec(memory_space=pltpu.SMEM)]
        + [pl.BlockSpec(memory_space=pl.ANY)] * len(blocks)
        + [pl.BlockSpec((TILE, depth), lambda i: (i, 0))],
        out_specs=pl.BlockSpec((rows, TILE), lambda i: (0, i)),
        out_shape=jax.ShapeDtypeStruct((rows, width), jnp.float32),
        scratch_shapes=[pltpu.VMEM((rows, depth), jnp.bfloat16), pltpu.SemaphoreType.DMA((len(pairs),))],
        compiler_params=pltpu.CompilerParams(vmem_limit_bytes=VMEM),
        cost_estimate=pl.CostEstimate(
            flops=2 * rows * depth * width, bytes_accessed=2 * depth * (width + rows) + 4 * rows * width, transcendentals=0
        ),
    )(core[None], *blocks, train)


def pick_kernel(spots, count, order, *refs):
    parts, away, keep, sems = refs[:count], *refs[count:]
    for slot in range(4):
        target = (away, keep)[slot // 2].at[pl.ds(slot % 2 * 128, 128)]
        for number, (part, block) in enumerate(spots):

            @pl.when(order[slot] == number)
            def _(slot=slot, part=part, block=block, target=target):
                pltpu.make_async_copy(parts[part].at[pl.ds(block * 128, 128)], target, sems.at[slot]).start()

    for slot in range(4):
        target = (away, keep)[slot // 2].at[pl.ds(slot % 2 * 128, 128)]
        pltpu.make_async_copy(parts[0].at[pl.ds(0, 128)], target, sems.at[slot]).wait()


def pick(order, parts, spots):
    width = parts[0].shape[1]
    half = jax.ShapeDtypeStruct((256, width), jnp.float32)
    return pl.pallas_call(
        functools.partial(pick_kernel, spots, len(parts)),
        in_specs=[pl.BlockSpec(memory_space=pltpu.SMEM)] + [pl.BlockSpec(memory_space=pl.ANY)] * len(parts),
        out_specs=[pl.BlockSpec(memory_space=pl.ANY)] * 2,
        out_shape=[half, half],
        scratch_shapes=[pltpu.SemaphoreType.DMA((4,))],
        compiler_params=pltpu.CompilerParams(vmem_limit_bytes=VMEM),
        cost_estimate=pl.CostEstimate(flops=0, bytes_accessed=8 * 512 * width, transcendentals=0),
    )(order, *parts)


def narrow_kernel(kept, got, message):
    total = kept[...] + got[...]
    peak = jnp.maximum(jnp.max(jnp.abs(total), axis=0, keepdims=True), 1e-30)
    power = 13.0 - jnp.floor(jnp.log2(peak))
    message[:128] = jnp.round(total * jnp.exp2(power)).astype(jnp.int32).astype(jnp.int16)
    message[128:] = jnp.broadcast_to(power, (16, power.shape[1])).astype(jnp.int32).astype(jnp.int16)


def narrow(kept, got):
    width = kept.shape[1]
    first = pl.BlockSpec((128, width), lambda i: (0, 0))
    return pl.pallas_call(
        narrow_kernel,
        grid=(1,),
        in_specs=[first, first],
        out_specs=pl.BlockSpec((144, width), lambda i: (0, 0)),
        out_shape=jax.ShapeDtypeStruct((144, width), jnp.int16),
        compiler_params=pltpu.CompilerParams(vmem_limit_bytes=VMEM),
        cost_estimate=pl.CostEstimate(flops=4 * 128 * width, bytes_accessed=10 * 128 * width, transcendentals=width),
    )(kept, got)


def widen(message):
    return message[:128].astype(jnp.float32) * jnp.exp2(-message[128:129].astype(jnp.float32))


def join(*values):
    return lax.optimization_barrier(values)


def shards(train_features, query_codes, query_exponents):
    layer, example = lax.axis_index("layer"), lax.axis_index("example")
    half, core = layer // 2, layer % 2
    z, low, y = example // 8, (example // 4) % 2, example % 4
    train = train_features[0]
    row_scale = jnp.exp2(-query_exponents[0].astype(jnp.float32))
    own = (query_codes[0].astype(jnp.float32) * row_scale[:, None]).astype(jnp.bfloat16)

    def by_core(zero, one):
        return jnp.where(core == 0, zero, one)

    wanted = jnp.stack([2 * (1 - half) + 1 - core, 2 * half + 1 - core, 2 * (1 - half) + core, 2 * half + core])
    steps = (wanted - z) % 4

    def order(zero, one):
        return by_core(jnp.array(zero, jnp.int32), jnp.array(one, jnp.int32))[steps]

    same = order([0, 1, 2, 3], [0, 1, 2, 3])
    crossed = order([0, 1, 2, 3], [0, 3, 2, 1])

    pair = send(own, PAIR)
    below, above = send(own, FIRST_UP), send(own, FIRST_DOWN)
    left, right = send(own, SECOND_UP), send(own, SECOND_DOWN)
    below_pair, above_pair = send(pair, FIRST_UP), send(pair, FIRST_DOWN)
    left_pair, right_pair = send(pair, SECOND_UP), send(pair, SECOND_DOWN)
    far = send(below, FIRST_UP)
    x0 = jnp.concatenate([own, pair], 0)
    x3 = jnp.concatenate([below, below_pair], 0)
    x1 = jnp.concatenate([above, above_pair], 0)
    up_1, down_1 = jnp.concatenate([left, left_pair], 0), jnp.concatenate([right, right_pair], 0)

    far_pair = send(above_pair, FIRST_DOWN)
    up_2, down_2 = send(x1, SECOND_UP), send(x1, SECOND_DOWN)
    up_3, down_3 = send(up_1, SECOND_UP), send(x3, SECOND_DOWN)
    part_a = products(core, [(x0, x0), (down_1, x1), (up_1, x3), (x1, down_1), (x3, up_1)], train)
    far_pair, up_2, down_2, up_3, down_3, part_a = join(far_pair, up_2, down_2, up_3, down_3, part_a)

    x2 = jnp.concatenate([far, far_pair], 0)
    up_4, down_5 = send(x2, SECOND_UP), send(by_core(down_3, x2), SECOND_DOWN)
    up_5, down_4 = send(x3, SECOND_UP), send(down_2, SECOND_DOWN)
    part_b = products(core, [(up_3, x2), (down_2, down_2), (up_2, down_3), (down_3, up_2), (x2, up_3)], train)
    up_4, down_5, up_5, down_4, part_b = join(up_4, down_5, up_5, down_4, part_b)

    away_0, keep_0 = pick(same, [part_a, part_b], [(0, 0), (0, 1), (1, 0), (0, 2)])
    up_6, down_6 = send(up_4, SECOND_UP), send(by_core(x2, down_3), SECOND_DOWN)
    got_0 = send(away_0, CORE)
    part_c = products(core, [(down_4, down_5), (down_5, up_4), (up_5, up_5), (up_4, down_4)], train)
    up_6, down_6, got_0, part_c = join(up_6, down_6, got_0, part_c)

    message_0 = narrow(keep_0, got_0)
    away_1, keep_1 = pick(same, [part_a, part_b, part_c], [(0, 3), (1, 1), (2, 0), (1, 2)])
    away_3, keep_3 = pick(same, [part_a, part_b, part_c], [(0, 4), (1, 3), (2, 1), (2, 2)])
    far_0, got_1, got_3 = send(message_0, ACROSS), send(away_1, CORE), send(away_3, CORE)
    part_d = products(core, [(down_6, down_6), (up_6, up_6)], train)
    got_1, got_3, part_d = join(got_1, got_3, part_d)

    message_1, message_3 = narrow(keep_1, got_1), narrow(keep_3, got_3)
    far_1, far_3 = send(message_1, ACROSS), send(message_3, ACROSS)
    away_2, keep_2 = pick(crossed, [part_b, part_c, part_d], [(0, 4), (2, 0), (2, 1), (1, 3)])
    got_2 = send(away_2, CORE)
    message_2 = narrow(keep_2, got_2)
    far_0, message_2 = join(far_0, message_2)
    far_2 = send(message_2, ACROSS)

    out = jnp.zeros((2, 4, 64, train.shape[0]), jnp.float32)
    for dy, keep, got, message in ((0, keep_0, got_0, far_0), (1, keep_1, got_1, far_1), (3, keep_3, got_3, far_3), (2, keep_2, got_2, far_2)):
        total = keep[128:] + got[128:] + widen(message)
        place_y = (y + dy) % 4
        out = lax.dynamic_update_slice(out, total[None, None, :64], (low, place_y, 0, 0))
        out = lax.dynamic_update_slice(out, total[None, None, 64:], (1 - low, place_y, 0, 0))
    return out.reshape(512, -1)


def solution(mesh):
    in_specs = (P("layer", "example", None), P("layer", "example", None), P("layer", "example"))
    out_specs = P("layer", "example")
    return jax.shard_map(shards, mesh=mesh, in_specs=in_specs, out_specs=out_specs, check_vma=False)
```

```python
import functools

import jax
import jax.numpy as jnp
from jax import lax
from jax.experimental import pallas as pl
from jax.experimental.pallas import tpu as pltpu
from jax.sharding import PartitionSpec as P

BOTH = ("layer", "example")


def moves(step):
    pairs = []
    for x in range(4):
        for core in range(2):
            for z in range(4):
                for y in range(4):
                    tx, tc, tz, ty = step(x, core, z, y)
                    pairs.append((place(x, core, z, y), place(tx % 4, tc % 2, tz % 4, ty % 4)))
    return pairs


def place(x, core, z, y):
    return (2 * (x // 2) + core) * 32 + (2 * z + x % 2) * 4 + y


FIRST_UP = moves(lambda x, c, z, y: (x, c, z + c, y + 1 - c))
FIRST_DOWN = moves(lambda x, c, z, y: (x, c, z - c, y - 1 + c))
SECOND_UP = moves(lambda x, c, z, y: (x, c, z + 1 - c, y + c))
SECOND_DOWN = moves(lambda x, c, z, y: (x, c, z - 1 + c, y - c))
PAIR = moves(lambda x, c, z, y: (x ^ 1, c, z, y))
CORE = moves(lambda x, c, z, y: (x, c + 1, z, y))
ACROSS = moves(lambda x, c, z, y: (x + 2, c, z, y))


def send(value, pairs):
    return lax.ppermute(value, BOTH, pairs)


TILE = 512


def product_kernel(choices, count, core, *refs):
    blocks, train, out, rows, sems = refs[:count], *refs[count:]

    @pl.when(pl.program_id(0) == 0)
    def _():
        for slot, pair in enumerate(choices):
            for number, choice in enumerate(pair):

                @pl.when(core[0] == number)
                def _(slot=slot, choice=choice):
                    pltpu.make_async_copy(blocks[choice], rows.at[pl.ds(slot * 128, 128)], sems.at[slot]).start()

        for slot in range(len(choices)):
            pltpu.make_async_copy(blocks[0], rows.at[pl.ds(slot * 128, 128)], sems.at[slot]).wait()

    out[...] = lax.dot_general(rows[...], train[...], (((1,), (1,)), ((), ())), preferred_element_type=jnp.float32)


def products(core, pairs, train):
    depth, width = train.shape[1], train.shape[0]
    blocks, choices = [], []
    for pair in pairs:
        spots = []
        for block in pair:
            found = [n for n, known in enumerate(blocks) if known is block]
            if not found:
                blocks.append(block)
            spots.append(found[0] if found else len(blocks) - 1)
        choices.append(spots)
    rows = 128 * len(pairs)
    return pl.pallas_call(
        functools.partial(product_kernel, choices, len(blocks)),
        grid=(width // TILE,),
        in_specs=[pl.BlockSpec(memory_space=pltpu.SMEM)]
        + [pl.BlockSpec(memory_space=pl.ANY)] * len(blocks)
        + [pl.BlockSpec((TILE, depth), lambda i: (i, 0))],
        out_specs=pl.BlockSpec((rows, TILE), lambda i: (0, i)),
        out_shape=jax.ShapeDtypeStruct((rows, width), jnp.float32),
        scratch_shapes=[pltpu.VMEM((rows, depth), jnp.bfloat16), pltpu.SemaphoreType.DMA((len(pairs),))],
        compiler_params=pltpu.CompilerParams(vmem_limit_bytes=40 * 2**20),
        cost_estimate=pl.CostEstimate(
            flops=2 * rows * depth * width, bytes_accessed=2 * depth * (width + rows) + 4 * rows * width, transcendentals=0
        ),
    )(core[None], *blocks, train)


def pick_kernel(spots, count, order, *refs):
    parts, away, keep, sems = refs[:count], *refs[count:]
    for slot in range(4):
        target = (away, keep)[slot // 2].at[pl.ds(slot % 2 * 128, 128)]
        for number, (part, block) in enumerate(spots):

            @pl.when(order[slot] == number)
            def _(slot=slot, part=part, block=block, target=target):
                pltpu.make_async_copy(parts[part].at[pl.ds(block * 128, 128)], target, sems.at[slot]).start()

    for slot in range(4):
        target = (away, keep)[slot // 2].at[pl.ds(slot % 2 * 128, 128)]
        pltpu.make_async_copy(parts[0].at[pl.ds(0, 128)], target, sems.at[slot]).wait()


def pick(order, parts, spots):
    width = parts[0].shape[1]
    half = jax.ShapeDtypeStruct((256, width), jnp.float32)
    return pl.pallas_call(
        functools.partial(pick_kernel, spots, len(parts)),
        in_specs=[pl.BlockSpec(memory_space=pltpu.SMEM)] + [pl.BlockSpec(memory_space=pl.ANY)] * len(parts),
        out_specs=[pl.BlockSpec(memory_space=pl.ANY)] * 2,
        out_shape=[half, half],
        scratch_shapes=[pltpu.SemaphoreType.DMA((4,))],
        compiler_params=pltpu.CompilerParams(vmem_limit_bytes=2 * 2**20),
        cost_estimate=pl.CostEstimate(flops=0, bytes_accessed=8 * 512 * width, transcendentals=0),
    )(order, *parts)


def narrow_kernel(kept, got, message):
    total = kept[...] + got[...]
    peak = jnp.maximum(jnp.max(jnp.abs(total), axis=0, keepdims=True), 1e-30)
    power = 13.0 - jnp.floor(jnp.log2(peak))
    message[:128] = jnp.round(total * jnp.exp2(power)).astype(jnp.int32).astype(jnp.int16)
    message[128:] = jnp.broadcast_to(power, (16, power.shape[1])).astype(jnp.int32).astype(jnp.int16)


def narrow(kept, got):
    width = kept.shape[1]
    first = pl.BlockSpec((128, width), lambda i: (0, 0))
    return pl.pallas_call(
        narrow_kernel,
        grid=(1,),
        in_specs=[first, first],
        out_specs=pl.BlockSpec((144, width), lambda i: (0, 0)),
        out_shape=jax.ShapeDtypeStruct((144, width), jnp.int16),
        compiler_params=pltpu.CompilerParams(vmem_limit_bytes=8 * 2**20),
        cost_estimate=pl.CostEstimate(flops=4 * 128 * width, bytes_accessed=10 * 128 * width, transcendentals=width),
    )(kept, got)


def widen(message):
    return message[:128].astype(jnp.float32) * jnp.exp2(-message[128:129].astype(jnp.float32))


def join(*values):
    return lax.optimization_barrier(values)


def shards(train_features, query_codes, query_exponents):
    layer, example = lax.axis_index("layer"), lax.axis_index("example")
    half, core = layer // 2, layer % 2
    z, low, y = example // 8, (example // 4) % 2, example % 4
    train = train_features[0]
    row_scale = jnp.exp2(-query_exponents[0].astype(jnp.float32))
    own = (query_codes[0].astype(jnp.float32) * row_scale[:, None]).astype(jnp.bfloat16)

    def by_core(zero, one):
        return jnp.where(core == 0, zero, one)

    wanted = jnp.stack([2 * (1 - half) + 1 - core, 2 * half + 1 - core, 2 * (1 - half) + core, 2 * half + core])
    order = (wanted - z) % 4

    pair = send(own, PAIR)
    below, above = send(own, FIRST_UP), send(own, FIRST_DOWN)
    left, right = send(own, SECOND_UP), send(own, SECOND_DOWN)
    below_pair, above_pair = send(pair, FIRST_UP), send(pair, FIRST_DOWN)
    left_pair, right_pair = send(pair, SECOND_UP), send(pair, SECOND_DOWN)
    far = send(below, FIRST_UP)
    x0 = jnp.concatenate([own, pair], 0)
    x3 = jnp.concatenate([below, below_pair], 0)
    x1 = jnp.concatenate([above, above_pair], 0)
    up_1, down_1 = jnp.concatenate([left, left_pair], 0), jnp.concatenate([right, right_pair], 0)

    far_pair = send(above_pair, FIRST_DOWN)
    up_2, down_2 = send(x1, SECOND_UP), send(x1, SECOND_DOWN)
    up_3, down_3 = send(up_1, SECOND_UP), send(x3, SECOND_DOWN)
    part_a = products(core, [(x0, x0), (down_1, x1), (up_1, x3), (x1, down_1), (x3, up_1)], train)
    far_pair, up_2, down_2, up_3, down_3, part_a = join(far_pair, up_2, down_2, up_3, down_3, part_a)

    x2 = jnp.concatenate([far, far_pair], 0)
    up_5, down_4 = send(x3, SECOND_UP), send(by_core(down_2, x2), SECOND_DOWN)
    part_b = products(core, [(up_3, x2), (down_2, down_2), (up_2, down_3), (down_3, up_2)], train)
    up_5, down_4, part_b = join(up_5, down_4, part_b)

    away_0, keep_0 = pick(order, [part_a, part_b], [(0, 0), (0, 1), (1, 0), (0, 2)])
    up_4, down_5 = send(x2, SECOND_UP), send(down_3, SECOND_DOWN)
    got_0 = send(away_0, CORE)
    part_c = products(core, [(down_4, down_4), (up_5, up_5), (x2, up_3)], train)
    up_4, down_5, got_0, part_c = join(up_4, down_5, got_0, part_c)

    message_0 = narrow(keep_0, got_0)
    message_0, order = join(message_0, order)
    away_1, keep_1 = pick(order, [part_a, part_b, part_c], [(0, 3), (1, 1), (2, 0), (1, 2)])
    up_6, down_6 = send(up_4, SECOND_UP), send(by_core(x2, down_2), SECOND_DOWN)
    got_1, far_0 = send(away_1, CORE), send(message_0, ACROSS)
    part_d = products(core, [(down_5, up_4), (up_4, down_5)], train)
    up_6, down_6, got_1, far_0, part_d = join(up_6, down_6, got_1, far_0, part_d)

    message_1, order = join(narrow(keep_1, got_1), order)
    away_3, keep_3 = pick(order, [part_a, part_b, part_c, part_d], [(0, 4), (1, 3), (3, 0), (2, 1)])
    got_3 = send(away_3, CORE)
    message_1, got_3 = join(message_1, got_3)
    far_1 = send(message_1, ACROSS)
    message_3 = narrow(keep_3, got_3)
    down_6, up_6, message_3 = join(down_6, up_6, message_3)
    far_3 = send(message_3, ACROSS)
    part_e = products(core, [(down_6, down_6), (up_6, up_6)], train)
    far_1, part_e = join(far_1, part_e)
    away_2, keep_2 = pick(order, [part_c, part_d, part_e], [(0, 2), (2, 0), (2, 1), (1, 1)])
    got_2 = send(away_2, CORE)
    message_2 = narrow(keep_2, got_2)
    keep_3, message_2 = join(keep_3, message_2)
    far_2 = send(message_2, ACROSS)

    out = jnp.zeros((2, 4, 64, train.shape[0]), jnp.float32)
    for dy, keep, got, message in ((0, keep_0, got_0, far_0), (1, keep_1, got_1, far_1), (3, keep_3, got_3, far_3), (2, keep_2, got_2, far_2)):
        total = keep[128:] + got[128:] + widen(message)
        place_y = (y + dy) % 4
        out = lax.dynamic_update_slice(out, total[None, None, :64], (low, place_y, 0, 0))
        out = lax.dynamic_update_slice(out, total[None, None, 64:], (1 - low, place_y, 0, 0))
    return out.reshape(512, -1)


def solution(mesh):
    in_specs = (P("layer", "example", None), P("layer", "example", None), P("layer", "example"))
    out_specs = P("layer", "example")
    return jax.shard_map(shards, mesh=mesh, in_specs=in_specs, out_specs=out_specs, check_vma=False)
```

```python
import functools

import jax
import jax.numpy as jnp
from jax import lax
from jax.experimental import pallas as pl
from jax.experimental.pallas import tpu as pltpu
from jax.sharding import PartitionSpec as P

BOTH = ("layer", "example")


def moves(step):
    pairs = []
    for x in range(4):
        for core in range(2):
            for z in range(4):
                for y in range(4):
                    tx, tc, tz, ty = step(x, core, z, y)
                    pairs.append((place(x, core, z, y), place(tx % 4, tc % 2, tz % 4, ty % 4)))
    return pairs


def place(x, core, z, y):
    return (2 * (x // 2) + core) * 32 + (2 * z + x % 2) * 4 + y


FIRST_UP = moves(lambda x, c, z, y: (x, c, z + c, y + 1 - c))
FIRST_DOWN = moves(lambda x, c, z, y: (x, c, z - c, y - 1 + c))
SECOND_UP = moves(lambda x, c, z, y: (x, c, z + 1 - c, y + c))
SECOND_DOWN = moves(lambda x, c, z, y: (x, c, z - 1 + c, y - c))
PAIR = moves(lambda x, c, z, y: (x ^ 1, c, z, y))
CORE = moves(lambda x, c, z, y: (x, c + 1, z, y))
ACROSS = moves(lambda x, c, z, y: (x + 2, c, z, y))


def send(value, pairs):
    return lax.ppermute(value, BOTH, pairs)


TILE = 512


def product_kernel(choices, count, core, *refs):
    blocks, train, out, rows, sems = refs[:count], *refs[count:]

    @pl.when(pl.program_id(0) == 0)
    def _():
        for slot, pair in enumerate(choices):
            for number, choice in enumerate(pair):

                @pl.when(core[0] == number)
                def _(slot=slot, choice=choice):
                    pltpu.make_async_copy(blocks[choice], rows.at[pl.ds(slot * 128, 128)], sems.at[slot]).start()

        for slot in range(len(choices)):
            pltpu.make_async_copy(blocks[0], rows.at[pl.ds(slot * 128, 128)], sems.at[slot]).wait()

    out[...] = lax.dot_general(rows[...], train[...], (((1,), (1,)), ((), ())), preferred_element_type=jnp.float32)


def products(core, pairs, train):
    depth, width = train.shape[1], train.shape[0]
    blocks, choices = [], []
    for pair in pairs:
        spots = []
        for block in pair:
            found = [n for n, known in enumerate(blocks) if known is block]
            if not found:
                blocks.append(block)
            spots.append(found[0] if found else len(blocks) - 1)
        choices.append(spots)
    rows = 128 * len(pairs)
    return pl.pallas_call(
        functools.partial(product_kernel, choices, len(blocks)),
        grid=(width // TILE,),
        in_specs=[pl.BlockSpec(memory_space=pltpu.SMEM)]
        + [pl.BlockSpec(memory_space=pl.ANY)] * len(blocks)
        + [pl.BlockSpec((TILE, depth), lambda i: (i, 0))],
        out_specs=pl.BlockSpec((rows, TILE), lambda i: (0, i)),
        out_shape=jax.ShapeDtypeStruct((rows, width), jnp.float32),
        scratch_shapes=[pltpu.VMEM((rows, depth), jnp.bfloat16), pltpu.SemaphoreType.DMA((len(pairs),))],
        compiler_params=pltpu.CompilerParams(vmem_limit_bytes=40 * 2**20),
        cost_estimate=pl.CostEstimate(
            flops=2 * rows * depth * width, bytes_accessed=2 * depth * (width + rows) + 4 * rows * width, transcendentals=0
        ),
    )(core[None], *blocks, train)


def pick_kernel(spots, count, order, *refs):
    parts, away, keep, sems = refs[:count], *refs[count:]
    for slot in range(4):
        target = (away, keep)[slot // 2].at[pl.ds(slot % 2 * 128, 128)]
        for number, (part, block) in enumerate(spots):

            @pl.when(order[slot] == number)
            def _(slot=slot, part=part, block=block, target=target):
                pltpu.make_async_copy(parts[part].at[pl.ds(block * 128, 128)], target, sems.at[slot]).start()

    for slot in range(4):
        target = (away, keep)[slot // 2].at[pl.ds(slot % 2 * 128, 128)]
        pltpu.make_async_copy(parts[0].at[pl.ds(0, 128)], target, sems.at[slot]).wait()


def pick(order, parts, spots):
    width = parts[0].shape[1]
    half = jax.ShapeDtypeStruct((256, width), jnp.float32)
    return pl.pallas_call(
        functools.partial(pick_kernel, spots, len(parts)),
        in_specs=[pl.BlockSpec(memory_space=pltpu.SMEM)] + [pl.BlockSpec(memory_space=pl.ANY)] * len(parts),
        out_specs=[pl.BlockSpec(memory_space=pl.ANY)] * 2,
        out_shape=[half, half],
        scratch_shapes=[pltpu.SemaphoreType.DMA((4,))],
        compiler_params=pltpu.CompilerParams(vmem_limit_bytes=2 * 2**20),
        cost_estimate=pl.CostEstimate(flops=0, bytes_accessed=8 * 512 * width, transcendentals=0),
    )(order, *parts)


def narrow_kernel(kept, got, message):
    total = kept[...] + got[...]
    peak = jnp.maximum(jnp.max(jnp.abs(total), axis=0, keepdims=True), 1e-30)
    power = 13.0 - jnp.floor(jnp.log2(peak))
    message[:128] = jnp.round(total * jnp.exp2(power)).astype(jnp.int32).astype(jnp.int16)
    message[128:] = jnp.broadcast_to(power, (16, power.shape[1])).astype(jnp.int32).astype(jnp.int16)


def narrow(kept, got):
    width = kept.shape[1]
    first = pl.BlockSpec((128, width), lambda i: (0, 0))
    return pl.pallas_call(
        narrow_kernel,
        grid=(1,),
        in_specs=[first, first],
        out_specs=pl.BlockSpec((144, width), lambda i: (0, 0)),
        out_shape=jax.ShapeDtypeStruct((144, width), jnp.int16),
        compiler_params=pltpu.CompilerParams(vmem_limit_bytes=8 * 2**20),
        cost_estimate=pl.CostEstimate(flops=4 * 128 * width, bytes_accessed=10 * 128 * width, transcendentals=width),
    )(kept, got)


def widen(message):
    return message[:128].astype(jnp.float32) * jnp.exp2(-message[128:129].astype(jnp.float32))


def join(*values):
    return lax.optimization_barrier(values)


def shards(train_features, query_codes, query_exponents):
    layer, example = lax.axis_index("layer"), lax.axis_index("example")
    half, core = layer // 2, layer % 2
    z, low, y = example // 8, (example // 4) % 2, example % 4
    train = train_features[0]
    row_scale = jnp.exp2(-query_exponents[0].astype(jnp.float32))
    own = (query_codes[0].astype(jnp.float32) * row_scale[:, None]).astype(jnp.bfloat16)

    def by_core(zero, one):
        return jnp.where(core == 0, zero, one)

    wanted = jnp.stack([2 * (1 - half) + 1 - core, 2 * half + 1 - core, 2 * (1 - half) + core, 2 * half + core])
    order = (wanted - z) % 4

    pair = send(own, PAIR)
    below, above = send(own, FIRST_UP), send(own, FIRST_DOWN)
    left, right = send(own, SECOND_UP), send(own, SECOND_DOWN)
    below_pair, above_pair = send(pair, FIRST_UP), send(pair, FIRST_DOWN)
    left_pair, right_pair = send(pair, SECOND_UP), send(pair, SECOND_DOWN)
    far = send(below, FIRST_UP)
    x0 = jnp.concatenate([own, pair], 0)
    x3 = jnp.concatenate([below, below_pair], 0)
    x1 = jnp.concatenate([above, above_pair], 0)
    up_1, down_1 = jnp.concatenate([left, left_pair], 0), jnp.concatenate([right, right_pair], 0)

    far_pair = send(above_pair, FIRST_DOWN)
    up_2, down_2 = send(x1, SECOND_UP), send(x1, SECOND_DOWN)
    up_3, down_3 = send(up_1, SECOND_UP), send(x3, SECOND_DOWN)
    part_a = products(core, [(x0, x0), (down_1, x1), (up_1, x3), (x1, down_1), (x3, up_1)], train)
    far_pair, up_2, down_2, up_3, down_3, part_a = join(far_pair, up_2, down_2, up_3, down_3, part_a)

    x2 = jnp.concatenate([far, far_pair], 0)
    up_5, down_4 = send(x3, SECOND_UP), send(by_core(down_2, x2), SECOND_DOWN)
    part_b = products(core, [(up_3, x2), (down_2, down_2), (up_2, down_3), (down_3, up_2)], train)
    up_5, down_4, part_b = join(up_5, down_4, part_b)

    away_0, keep_0 = pick(order, [part_a, part_b], [(0, 0), (0, 1), (1, 0), (0, 2)])
    up_4, down_5 = send(x2, SECOND_UP), send(down_3, SECOND_DOWN)
    got_0 = send(away_0, CORE)
    part_c = products(core, [(down_4, down_4), (up_5, up_5), (x2, up_3)], train)
    up_4, down_5, got_0, part_c = join(up_4, down_5, got_0, part_c)

    message_0 = narrow(keep_0, got_0)
    message_0, order = join(message_0, order)
    away_1, keep_1 = pick(order, [part_a, part_b, part_c], [(0, 3), (1, 1), (2, 0), (1, 2)])
    up_6, down_6 = send(up_4, SECOND_UP), send(by_core(x2, down_2), SECOND_DOWN)
    got_1, far_0 = send(away_1, CORE), send(message_0, ACROSS)
    part_d = products(core, [(down_5, up_4), (up_4, down_5)], train)
    up_6, down_6, got_1, far_0, part_d = join(up_6, down_6, got_1, far_0, part_d)

    message_1, order = join(narrow(keep_1, got_1), order)
    away_3, keep_3 = pick(order, [part_a, part_b, part_c, part_d], [(0, 4), (1, 3), (3, 0), (2, 1)])
    message_1, away_3 = join(message_1, away_3)
    got_3 = send(away_3, CORE)
    far_1 = send(message_1, ACROSS)
    message_3 = narrow(keep_3, got_3)
    down_6, up_6, message_3 = join(down_6, up_6, message_3)
    far_3 = send(message_3, ACROSS)
    part_e = products(core, [(down_6, down_6), (up_6, up_6)], train)
    far_1, part_e, far_0 = join(far_1, part_e, far_0)
    away_2, keep_2 = pick(order, [part_c, part_d, part_e], [(0, 2), (2, 0), (2, 1), (1, 1)])
    got_2 = send(away_2, CORE)
    message_2 = narrow(keep_2, got_2)
    far_2 = send(message_2, ACROSS)
    keep_3, far_2 = join(keep_3, far_2)

    out = jnp.zeros((2, 4, 64, train.shape[0]), jnp.float32)
    for dy, keep, got, message in ((0, keep_0, got_0, far_0), (1, keep_1, got_1, far_1), (3, keep_3, got_3, far_3), (2, keep_2, got_2, far_2)):
        total = keep[128:] + got[128:] + widen(message)
        place_y = (y + dy) % 4
        out = lax.dynamic_update_slice(out, total[None, None, :64], (low, place_y, 0, 0))
        out = lax.dynamic_update_slice(out, total[None, None, 64:], (1 - low, place_y, 0, 0))
    return out.reshape(512, -1)


def solution(mesh):
    in_specs = (P("layer", "example", None), P("layer", "example", None), P("layer", "example"))
    out_specs = P("layer", "example")
    return jax.shard_map(shards, mesh=mesh, in_specs=in_specs, out_specs=out_specs, check_vma=False)
```

```python
import functools

import jax
import jax.numpy as jnp
from jax import lax
from jax.experimental import pallas as pl
from jax.experimental.pallas import tpu as pltpu
from jax.sharding import PartitionSpec as P

BOTH = ("layer", "example")


def moves(step):
    pairs = []
    for x in range(4):
        for core in range(2):
            for z in range(4):
                for y in range(4):
                    tx, tc, tz, ty = step(x, core, z, y)
                    pairs.append((place(x, core, z, y), place(tx % 4, tc % 2, tz % 4, ty % 4)))
    return pairs


def place(x, core, z, y):
    return (2 * (x // 2) + core) * 32 + (2 * z + x % 2) * 4 + y


FIRST_UP = moves(lambda x, c, z, y: (x, c, z + c, y + 1 - c))
FIRST_DOWN = moves(lambda x, c, z, y: (x, c, z - c, y - 1 + c))
SECOND_UP = moves(lambda x, c, z, y: (x, c, z + 1 - c, y + c))
SECOND_DOWN = moves(lambda x, c, z, y: (x, c, z - 1 + c, y - c))
PAIR = moves(lambda x, c, z, y: (x ^ 1, c, z, y))
CORE = moves(lambda x, c, z, y: (x, c + 1, z, y))
ACROSS = moves(lambda x, c, z, y: (x + 2, c, z, y))


def send(value, pairs):
    return lax.ppermute(value, BOTH, pairs)


TILE = 768


def product_kernel(choices, count, core, *refs):
    blocks, train, out, rows, sems = refs[:count], *refs[count:]

    @pl.when(pl.program_id(0) == 0)
    def _():
        for slot, pair in enumerate(choices):
            for number, choice in enumerate(pair):

                @pl.when(core[0] == number)
                def _(slot=slot, choice=choice):
                    pltpu.make_async_copy(blocks[choice], rows.at[pl.ds(slot * 128, 128)], sems.at[slot]).start()

        for slot in range(len(choices)):
            pltpu.make_async_copy(blocks[0], rows.at[pl.ds(slot * 128, 128)], sems.at[slot]).wait()

    out[...] = lax.dot_general(rows[...], train[...], (((1,), (1,)), ((), ())), preferred_element_type=jnp.float32)


def products(core, pairs, train):
    depth, width = train.shape[1], train.shape[0]
    blocks, choices = [], []
    for pair in pairs:
        spots = []
        for block in pair:
            found = [n for n, known in enumerate(blocks) if known is block]
            if not found:
                blocks.append(block)
            spots.append(found[0] if found else len(blocks) - 1)
        choices.append(spots)
    rows = 128 * len(pairs)
    return pl.pallas_call(
        functools.partial(product_kernel, choices, len(blocks)),
        grid=(width // TILE,),
        in_specs=[pl.BlockSpec(memory_space=pltpu.SMEM)]
        + [pl.BlockSpec(memory_space=pl.ANY)] * len(blocks)
        + [pl.BlockSpec((TILE, depth), lambda i: (i, 0))],
        out_specs=pl.BlockSpec((rows, TILE), lambda i: (0, i)),
        out_shape=jax.ShapeDtypeStruct((rows, width), jnp.float32),
        scratch_shapes=[pltpu.VMEM((rows, depth), jnp.bfloat16), pltpu.SemaphoreType.DMA((len(pairs),))],
        compiler_params=pltpu.CompilerParams(vmem_limit_bytes=40 * 2**20),
        cost_estimate=pl.CostEstimate(
            flops=2 * rows * depth * width, bytes_accessed=2 * depth * (width + rows) + 4 * rows * width, transcendentals=0
        ),
    )(core[None], *blocks, train)


def pick_kernel(spots, count, order, *refs):
    parts, away, keep, sems = refs[:count], *refs[count:]
    for slot in range(4):
        target = (away, keep)[slot // 2].at[pl.ds(slot % 2 * 128, 128)]
        for number, (part, block) in enumerate(spots):

            @pl.when(order[slot] == number)
            def _(slot=slot, part=part, block=block, target=target):
                pltpu.make_async_copy(parts[part].at[pl.ds(block * 128, 128)], target, sems.at[slot]).start()

    for slot in range(4):
        target = (away, keep)[slot // 2].at[pl.ds(slot % 2 * 128, 128)]
        pltpu.make_async_copy(parts[0].at[pl.ds(0, 128)], target, sems.at[slot]).wait()


def pick(order, parts, spots):
    width = parts[0].shape[1]
    half = jax.ShapeDtypeStruct((256, width), jnp.float32)
    return pl.pallas_call(
        functools.partial(pick_kernel, spots, len(parts)),
        in_specs=[pl.BlockSpec(memory_space=pltpu.SMEM)] + [pl.BlockSpec(memory_space=pl.ANY)] * len(parts),
        out_specs=[pl.BlockSpec(memory_space=pl.ANY)] * 2,
        out_shape=[half, half],
        scratch_shapes=[pltpu.SemaphoreType.DMA((4,))],
        compiler_params=pltpu.CompilerParams(vmem_limit_bytes=2 * 2**20),
        cost_estimate=pl.CostEstimate(flops=0, bytes_accessed=8 * 512 * width, transcendentals=0),
    )(order, *parts)


def narrow_kernel(kept, got, message):
    total = kept[...] + got[...]
    peak = jnp.maximum(jnp.max(jnp.abs(total), axis=0, keepdims=True), 1e-30)
    power = 13.0 - jnp.floor(jnp.log2(peak))
    message[:128] = jnp.round(total * jnp.exp2(power)).astype(jnp.int32).astype(jnp.int16)
    message[128:] = jnp.broadcast_to(power, (16, power.shape[1])).astype(jnp.int32).astype(jnp.int16)


def narrow(kept, got):
    width = kept.shape[1]
    first = pl.BlockSpec((128, width), lambda i: (0, 0))
    return pl.pallas_call(
        narrow_kernel,
        grid=(1,),
        in_specs=[first, first],
        out_specs=pl.BlockSpec((144, width), lambda i: (0, 0)),
        out_shape=jax.ShapeDtypeStruct((144, width), jnp.int16),
        compiler_params=pltpu.CompilerParams(vmem_limit_bytes=8 * 2**20),
        cost_estimate=pl.CostEstimate(flops=4 * 128 * width, bytes_accessed=10 * 128 * width, transcendentals=width),
    )(kept, got)


def widen(message):
    return message[:128].astype(jnp.float32) * jnp.exp2(-message[128:129].astype(jnp.float32))


def join(*values):
    return lax.optimization_barrier(values)


def shards(train_features, query_codes, query_exponents):
    layer, example = lax.axis_index("layer"), lax.axis_index("example")
    half, core = layer // 2, layer % 2
    z, low, y = example // 8, (example // 4) % 2, example % 4
    train = train_features[0]
    row_scale = jnp.exp2(-query_exponents[0].astype(jnp.float32))
    own = (query_codes[0].astype(jnp.float32) * row_scale[:, None]).astype(jnp.bfloat16)

    def by_core(zero, one):
        return jnp.where(core == 0, zero, one)

    wanted = jnp.stack([2 * (1 - half) + 1 - core, 2 * half + 1 - core, 2 * (1 - half) + core, 2 * half + core])
    order = (wanted - z) % 4

    pair = send(own, PAIR)
    below, above = send(own, FIRST_UP), send(own, FIRST_DOWN)
    left, right = send(own, SECOND_UP), send(own, SECOND_DOWN)
    below_pair, above_pair = send(pair, FIRST_UP), send(pair, FIRST_DOWN)
    left_pair, right_pair = send(pair, SECOND_UP), send(pair, SECOND_DOWN)
    far = send(below, FIRST_UP)
    x0 = jnp.concatenate([own, pair], 0)
    x3 = jnp.concatenate([below, below_pair], 0)
    x1 = jnp.concatenate([above, above_pair], 0)
    up_1, down_1 = jnp.concatenate([left, left_pair], 0), jnp.concatenate([right, right_pair], 0)

    far_pair = send(above_pair, FIRST_DOWN)
    up_2, down_2 = send(x1, SECOND_UP), send(x1, SECOND_DOWN)
    up_3, down_3 = send(up_1, SECOND_UP), send(x3, SECOND_DOWN)
    part_a = products(core, [(x0, x0), (down_1, x1), (up_1, x3), (x1, down_1), (x3, up_1)], train)
    far_pair, up_2, down_2, up_3, down_3, part_a = join(far_pair, up_2, down_2, up_3, down_3, part_a)

    x2 = jnp.concatenate([far, far_pair], 0)
    up_5, down_4 = send(x3, SECOND_UP), send(by_core(down_2, x2), SECOND_DOWN)
    part_b = products(core, [(up_3, x2), (down_2, down_2), (up_2, down_3), (down_3, up_2)], train)
    up_5, down_4, part_b = join(up_5, down_4, part_b)

    away_0, keep_0 = pick(order, [part_a, part_b], [(0, 0), (0, 1), (1, 0), (0, 2)])
    up_4, down_5 = send(x2, SECOND_UP), send(down_3, SECOND_DOWN)
    got_0 = send(away_0, CORE)
    part_c = products(core, [(down_4, down_4), (up_5, up_5), (x2, up_3)], train)
    up_4, down_5, got_0, part_c = join(up_4, down_5, got_0, part_c)

    message_0 = narrow(keep_0, got_0)
    message_0, order = join(message_0, order)
    away_1, keep_1 = pick(order, [part_a, part_b, part_c], [(0, 3), (1, 1), (2, 0), (1, 2)])
    up_6, down_6 = send(up_4, SECOND_UP), send(by_core(x2, down_2), SECOND_DOWN)
    got_1, far_0 = send(away_1, CORE), send(message_0, ACROSS)
    part_d = products(core, [(down_5, up_4), (up_4, down_5)], train)
    up_6, down_6, got_1, far_0, part_d = join(up_6, down_6, got_1, far_0, part_d)

    message_1, order = join(narrow(keep_1, got_1), order)
    away_3, keep_3 = pick(order, [part_a, part_b, part_c, part_d], [(0, 4), (1, 3), (3, 0), (2, 1)])
    message_1, away_3 = join(message_1, away_3)
    got_3 = send(away_3, CORE)
    far_1 = send(message_1, ACROSS)
    message_3 = narrow(keep_3, got_3)
    down_6, up_6, message_3 = join(down_6, up_6, message_3)
    far_3 = send(message_3, ACROSS)
    part_e = products(core, [(down_6, down_6), (up_6, up_6)], train)
    far_1, part_e, far_0 = join(far_1, part_e, far_0)
    away_2, keep_2 = pick(order, [part_c, part_d, part_e], [(0, 2), (2, 0), (2, 1), (1, 1)])
    got_2 = send(away_2, CORE)
    message_2 = narrow(keep_2, got_2)
    far_2 = send(message_2, ACROSS)
    keep_3, far_2 = join(keep_3, far_2)

    out = jnp.zeros((2, 4, 64, train.shape[0]), jnp.float32)
    for dy, keep, got, message in ((0, keep_0, got_0, far_0), (1, keep_1, got_1, far_1), (3, keep_3, got_3, far_3), (2, keep_2, got_2, far_2)):
        total = keep[128:] + got[128:] + widen(message)
        place_y = (y + dy) % 4
        out = lax.dynamic_update_slice(out, total[None, None, :64], (low, place_y, 0, 0))
        out = lax.dynamic_update_slice(out, total[None, None, 64:], (1 - low, place_y, 0, 0))
    return out.reshape(512, -1)


def solution(mesh):
    in_specs = (P("layer", "example", None), P("layer", "example", None), P("layer", "example"))
    out_specs = P("layer", "example")
    return jax.shard_map(shards, mesh=mesh, in_specs=in_specs, out_specs=out_specs, check_vma=False)
```
